32 devices in a mesh: parts: 2 (over y), rows: 4 (over z), cols: 2 (over x), sub: 2 (over core).
Axes of the slice: x: 2, y: 2, z: 4, core: 2. Of those that a mesh axis runs over, the one named last changes fastest.
Arguments:
- left_states: float32 [32, 2, 65536], P(('parts', 'rows', 'cols', 'sub')), parts along dimension 0, may hold values from -6 to 6
- right_states: float32 [32, 2, 65536], P(('parts', 'rows', 'cols', 'sub')), parts along dimension 0, may hold values from -6 to 6
- gates: float32 [4, 2, 128, 128], P('parts'), parts along dimension 0, may hold values from -0.375 to 0.375
- left_index: int32 [2048], P('parts'), parts along dimension 0, may hold values from 0 to 65535
- right_index: int32 [2048], P('parts'), parts along dimension 0, may hold values from 0 to 65535
Outputs:
- amplitudes: float32 [4, 1024, 1024], P('parts', 'rows', ('cols', 'sub')), parts along dimension 0
The draws below stay inside these ranges and needn't reach their ends.
There are 2 independent parts, one for each index of `parts`. The reference program is written for one: setup_inputs(seed, part) draws one part's arguments, and reference() takes and returns one part's arrays. A program takes and returns all parts, laid end to end along the dimension named above; each array names one. Nothing has to cross between parts.
All inputs are finite; a program needn't handle non-finite values.
Results may differ from the reference program's by a relative error of at most 0.000073.
Values sent between devices are 32-bit elements; how exact they have to be, the bound alone decides.
A program may use at most 64 MiB of HBM per device.

```python
import jax
import jax.numpy as jnp
from jax import lax

GATE = 128
SLAB = 65536
PATHS = 16
NLEFT = 1024
NRIGHT = 1024


def plant(result, own_key, least, largest):
    dims = result.shape
    spot = [jax.random.randint(jax.random.fold_in(own_key, axis), (), 0, dims[axis]) for axis in range(len(dims))]
    result = result.at[tuple(spot)].set(least)
    longest = dims.index(max(dims))
    spot[longest] = (spot[longest] + 1) % dims[longest]
    return result.at[tuple(spot)].set(largest)


def level_of(rng, extent, cuts, low, largest):
    loudness, own = 1.0, jax.random.fold_in(rng, 6)
    for position, blocks in cuts:
        draws = jnp.exp(jax.random.uniform(jax.random.fold_in(own, position), (blocks,), jnp.float32, low / len(cuts), largest / len(cuts)))
        loudness = loudness * jnp.repeat(draws, extent[position] // blocks).reshape([-1 if axis == position else 1 for axis in range(len(extent))])
    return loudness


def centred(key, dims, scale, limit, shards=(), held_as=jnp.bfloat16):
    level = level_of(key, dims, shards, -0.22, 0.18) if shards else 1.0
    values = jax.random.normal(key, dims, jnp.float32) * scale * level
    return jnp.minimum(jnp.maximum(values, -limit), limit).astype(held_as)


def setup_inputs(seed: int = 0, part: int = 0) -> dict:
    key_list = jax.random.split(jax.random.key(seed), 6)
    part_splits = jax.random.split(jax.random.fold_in(key_list[5], part), 6)
    left_states = centred(part_splits[0], (PATHS, 2, SLAB), 1.0, 6.0, ((0, 16),), jnp.float32)
    right_states = centred(part_splits[1], (PATHS, 2, SLAB), 1.0, 6.0, ((0, 16),), jnp.float32)
    gates = centred(part_splits[2], (2, 2, GATE, GATE), (2 * GATE) ** -0.5, 0.375, (), jnp.float32)
    left_index = plant(jax.random.randint(part_splits[3], (NLEFT,), 0, SLAB), jax.random.fold_in(part_splits[3], 1), 0, SLAB - 1).astype(jnp.int32)
    right_index = plant(jax.random.randint(part_splits[4], (NRIGHT,), 0, SLAB), jax.random.fold_in(part_splits[4], 1), 0, SLAB - 1).astype(jnp.int32)
    return {"left_states": left_states, "right_states": right_states, "gates": gates, "left_index": left_index, "right_index": right_index}


def apply_layers(states, gates):
    highest = lax.Precision.HIGHEST
    count = states.shape[0]
    real = states[:, 0].reshape(count, -1, GATE)
    imag = states[:, 1].reshape(count, -1, GATE)
    u_real, u_imag = (gates[0, 0], gates[0, 1])
    new_real = jnp.einsum('nag,hg->nah', real, u_real, precision=highest) - jnp.einsum('nag,hg->nah', imag, u_imag, precision=highest)
    new_imag = jnp.einsum('nag,hg->nah', real, u_imag, precision=highest) + jnp.einsum('nag,hg->nah', imag, u_real, precision=highest)
    real = new_real.reshape(count, -1, GATE, GATE)
    imag = new_imag.reshape(count, -1, GATE, GATE)
    v_real, v_imag = (gates[1, 0], gates[1, 1])
    out_real = jnp.einsum('qm,nhml->nhql', v_real, real, precision=highest) - jnp.einsum('qm,nhml->nhql', v_imag, imag, precision=highest)
    out_imag = jnp.einsum('qm,nhml->nhql', v_imag, real, precision=highest) + jnp.einsum('qm,nhml->nhql', v_real, imag, precision=highest)
    return (out_real.reshape(count, -1), out_imag.reshape(count, -1))

def pick_values(states, gates, index):
    real, imag = apply_layers(states, gates)
    return jnp.stack([jnp.take(real, index, axis=1), jnp.take(imag, index, axis=1)])

def transposed_product(first, second):
    return lax.dot_general(first, second, (((0,), (0,)), ((), ())), precision=lax.Precision.HIGHEST, preferred_element_type=jnp.float32)

def reference(left_states, right_states, gates, left_index, right_index):
    blocks = PATHS // 8

    def one_block(pair):
        left_block, right_block = pair
        return (pick_values(left_block, gates, left_index), pick_values(right_block, gates, right_index))
    left_pick, right_pick = lax.map(one_block, (left_states.reshape(blocks, 8, 2, SLAB), right_states.reshape(blocks, 8, 2, SLAB)))
    left_pick = jnp.transpose(left_pick, (1, 0, 2, 3)).reshape(2, PATHS, NLEFT)
    right_pick = jnp.transpose(right_pick, (1, 0, 2, 3)).reshape(2, PATHS, NRIGHT)
    out_real = transposed_product(left_pick[0], right_pick[0]) - transposed_product(left_pick[1], right_pick[1])
    out_imag = transposed_product(left_pick[0], right_pick[1]) + transposed_product(left_pick[1], right_pick[0])
    scale = jnp.float32(1.0) / jnp.sqrt(jnp.float32(PATHS))
    return jnp.stack([out_real, out_imag]) * scale
```

```python
import functools
import math

import jax
import jax.numpy as jnp
from jax import lax
from jax.experimental import pallas as pl
from jax.experimental.pallas import tpu as pltpu
from jax.sharding import PartitionSpec as P

MESH = pl.DeviceIdType.MESH
BF16 = jnp.bfloat16
F32 = jnp.float32


def split(x):
    high = x.astype(BF16)
    return high, (x - high.astype(F32)).astype(BF16)


def dot(a, b, dims=((1,), (0,))):
    return lax.dot_general(a, b, (dims, ((), ())), preferred_element_type=F32)


def for_blocks(count, body):
    if count <= 4:
        for b in range(count):
            body(b)
    else:

        def step(b, carry):
            body(b)
            return carry

        lax.fori_loop(0, count, step, 0)


def half_picks(state_ref, p, gate, second, index_ref, width, picked_ref, emit):
    size = gate[0].shape[0] // 2
    rows = state_ref.shape[1] // 2
    slabs = rows // size
    real = state_ref[p, pl.ds(0, rows, stride=2), :]
    imag = state_ref[p, pl.ds(1, rows, stride=2), :]
    xh, xl = split(jnp.concatenate([real, imag], axis=1))
    gh, gl = gate
    nt = ((1,), (1,))
    first = dot(xh, gh, nt) + (dot(xl, gh, nt) + dot(xh, gl, nt))
    parts = [
        jnp.concatenate(
            [first[h * size : (h + 1) * size, c * size : (c + 1) * size] for h in range(slabs)], axis=1
        )
        for c in range(2)
    ]
    high, low = split(jnp.concatenate(parts, axis=0))
    picked_ref[: 2 * size, :] = high
    picked_ref[2 * size :, :] = low

    def body(b):
        at = b * width if isinstance(b, int) else pl.multiple_of(b * width, width)
        index = index_ref[:, pl.ds(at, width)]
        low_bits = lax.rem(index, size)
        mid = lax.rem(lax.div(index, size), size)
        column = lax.div(index, size * size) * size + low_bits
        spot = lax.broadcasted_iota(jnp.int32, (slabs * size, width), 0)
        hot = jnp.where(spot == column, 1.0, 0.0).astype(BF16)
        found = dot(picked_ref[...], hot)
        found = found[: 2 * size] + found[2 * size :]
        spot = lax.broadcasted_iota(jnp.int32, (size, width), 0)
        hot = jnp.where(spot == mid, 1.0, 0.0).astype(BF16)
        rows2 = dot(second, jnp.concatenate([hot, hot], axis=0))
        fr, fi = found[:size], found[size:]
        vr, vi = rows2[:size], rows2[size:]
        out_r = jnp.sum(vr * fr - vi * fi, axis=0, keepdims=True)
        out_i = jnp.sum(vr * fi + vi * fr, axis=0, keepdims=True)
        lanes = width // 128
        emit(
            b,
            jnp.concatenate(
                [o[:, k * 128 : (k + 1) * 128] for o in (out_r, out_i) for k in range(lanes)], axis=0
            ),
        )

    for_blocks(index_ref.shape[1] // width, body)


def kernel(
    counts,
    left_ref,
    right_ref,
    gates_ref,
    left_index_ref,
    right_index_ref,
    out_ref,
    left_buf,
    right_buf,
    picked,
    send,
    recv,
    load_sem,
    send_sem,
    recv_sem,
):
    row_count, col_count, sub_count = counts
    group = col_count * sub_count
    n = row_count * group
    held = left_buf.shape[0]
    tile_l = left_index_ref.shape[1] // row_count
    tile_r = right_index_ref.shape[1] // group
    rows_l = 2 * tile_l // 128
    rows_r = 2 * tile_r // 128
    unit = rows_l + rows_r
    slot = held * unit
    me = (lax.axis_index("rows") * col_count + lax.axis_index("cols")) * sub_count + lax.axis_index("sub")

    load_l = pltpu.make_async_copy(left_ref, left_buf, load_sem.at[0])
    load_r = pltpu.make_async_copy(right_ref, right_buf, load_sem.at[1])
    load_l.start()
    load_r.start()

    def peer(offset):
        d = lax.rem(me + offset, n)
        where = {
            "rows": lax.div(d, group),
            "cols": lax.rem(lax.div(d, sub_count), col_count),
            "sub": lax.rem(d, sub_count),
        }
        return d, where

    barrier = pltpu.get_barrier_semaphore()

    def greet(offset, carry):
        pl.semaphore_signal(barrier, inc=1, device_id=peer(offset)[1], device_id_type=MESH)
        return carry

    lax.fori_loop(1, n, greet, 0)

    ur, ui = gates_ref[0, 0], gates_ref[0, 1]
    gate = split(
        jnp.concatenate(
            [jnp.concatenate([ur, -ui], axis=1), jnp.concatenate([ui, ur], axis=1)], axis=0
        )
    )
    second = jnp.concatenate(
        split(jnp.concatenate([gates_ref[1, 0].T, gates_ref[1, 1].T], axis=0)), axis=1
    )
    scale = 1.0 / math.sqrt(n * held)

    load_l.wait()
    for p in range(held):

        def emit_left(b, rows, p=p):
            rows = rows * scale
            for g in range(group):
                send[b * group + g, p * unit : p * unit + rows_l, :] = rows

        half_picks(left_buf, p, gate, second, left_index_ref, tile_l, picked, emit_left)
    load_r.wait()
    for p in range(held):

        def emit_right(b, rows, p=p):
            for r in range(row_count):
                send[r * group + b, p * unit + rows_l : (p + 1) * unit, :] = rows

        half_picks(right_buf, p, gate, second, right_index_ref, tile_r, picked, emit_right)

    pl.semaphore_wait(barrier, n - 1)

    def place(d):
        return recv.at[pl.ds(pl.multiple_of(d * slot, slot), slot), :]

    def push(offset, carry):
        d, where = peer(offset)
        pltpu.make_async_remote_copy(
            src_ref=send.at[d],
            dst_ref=place(me),
            send_sem=send_sem,
            recv_sem=recv_sem,
            device_id=where,
            device_id_type=MESH,
        ).start()
        return carry

    lax.fori_loop(1, n, push, 0)
    recv[pl.ds(pl.multiple_of(me * slot, slot), slot), :] = send[me]
    everything = recv.at[pl.ds(0, (n - 1) * slot), :]
    pltpu.make_async_copy(everything, everything, recv_sem).wait()

    def take(start, rows):
        return jnp.concatenate(
            [recv[pl.ds(start + t, n * held, stride=unit), :] for t in range(rows)], axis=1
        )

    lr, li = take(0, rows_l // 2), take(rows_l // 2, rows_l // 2)
    rr, ri = take(rows_l, rows_r // 2), take(rows_l + rows_r // 2, rows_r // 2)
    lh, ll = split(jnp.concatenate([lr, li], axis=0))
    rh, rl = split(
        jnp.concatenate(
            [jnp.concatenate([rr, -ri], axis=0), jnp.concatenate([ri, rr], axis=0)], axis=1
        )
    )
    left = jnp.concatenate([lh, lh, ll], axis=0)
    right = jnp.concatenate([rh, rl, rh], axis=0)
    result = dot(left, right, ((0,), (0,)))
    out_ref[0] = result[:, :tile_r]
    out_ref[1] = result[:, tile_r:]
    sent = send.at[pl.ds(0, n - 1)]
    pltpu.make_async_copy(sent, sent, send_sem).wait()


def per_device(counts, left_states, right_states, gates, left_index, right_index):
    row_count, col_count, sub_count = counts
    group = col_count * sub_count
    n = row_count * group
    size = gates.shape[-1]
    held = left_states.shape[0]
    nleft, nright = left_index.shape[0], right_index.shape[0]
    tile_l, tile_r = nleft // row_count, nright // group
    unit = 2 * (tile_l + tile_r) // 128
    slab = left_states.shape[2]

    def rows_of(states):
        return states.reshape(held, 2, slab // size, size).transpose(0, 2, 1, 3).reshape(held, -1, size)

    vmem = pl.BlockSpec(memory_space=pltpu.VMEM)
    hbm = pl.BlockSpec(memory_space=pl.ANY)
    return pl.pallas_call(
        functools.partial(kernel, counts),
        out_shape=jax.ShapeDtypeStruct((2, tile_l, tile_r), F32),
        in_specs=[hbm, hbm, vmem, vmem, vmem],
        out_specs=vmem,
        scratch_shapes=[
            pltpu.VMEM((held, 2 * slab // size, size), F32),
            pltpu.VMEM((held, 2 * slab // size, size), F32),
            pltpu.VMEM((4 * size, slab // size), BF16),
            pltpu.VMEM((n, held * unit, 128), F32),
            pltpu.VMEM((n * held * unit, 128), F32),
            pltpu.SemaphoreType.DMA((2,)),
            pltpu.SemaphoreType.DMA,
            pltpu.SemaphoreType.DMA,
        ],
        compiler_params=pltpu.CompilerParams(
            collective_id=0, has_side_effects=True, vmem_limit_bytes=40 * 1024 * 1024
        ),
    )(
        rows_of(left_states),
        rows_of(right_states),
        gates,
        left_index.reshape(1, nleft),
        right_index.reshape(1, nright),
    )


def solution(mesh):
    counts = tuple(mesh.shape[a] for a in ("rows", "cols", "sub"))
    return jax.shard_map(
        functools.partial(per_device, counts),
        mesh=mesh,
        in_specs=(
            P(("parts", "rows", "cols", "sub"), None, None),
            P(("parts", "rows", "cols", "sub"), None, None),
            P("parts", None, None, None),
            P("parts"),
            P("parts"),
        ),
        out_specs=P("parts", "rows", ("cols", "sub")),
        check_vma=False,
    )
```

```python
import functools
import math

import jax
import jax.numpy as jnp
from jax import lax
from jax.experimental import pallas as pl
from jax.experimental.pallas import tpu as pltpu
from jax.sharding import PartitionSpec as P

MESH = pl.DeviceIdType.MESH
BF16 = jnp.bfloat16
F32 = jnp.float32


def split(x):
    high = x.astype(BF16)
    return high, (x - high.astype(F32)).astype(BF16)


def dot(a, b, dims=((1,), (0,))):
    return lax.dot_general(a, b, (dims, ((), ())), preferred_element_type=F32)


def for_blocks(count, body):
    if count <= 4:
        for b in range(count):
            body(b)
    else:

        def step(b, carry):
            body(b)
            return carry

        lax.fori_loop(0, count, step, 0)


def block(b, width):
    start = b * width
    return pl.ds(start if isinstance(start, int) else pl.multiple_of(start, width), width)


def prepare(index_ref, width, size, slabs, hot_ref, mid_ref):
    shift = size.bit_length() - 1

    def body(b):
        cols = block(b, width)
        index = index_ref[:, cols]
        column = ((index >> (2 * shift)) << shift) | (index & (size - 1))
        mid = (index >> shift) & (size - 1)
        spot = lax.broadcasted_iota(jnp.int32, (slabs * size, width), 0)
        hot_ref[:, cols] = jnp.where(spot == column, 1.0, 0.0).astype(BF16)
        spot = lax.broadcasted_iota(jnp.int32, (size, width), 0)
        mid_ref[:, cols] = jnp.where(spot == mid, 1.0, 0.0).astype(BF16)

    for_blocks(index_ref.shape[1] // width, body)


def gather_rows(second, width, mid_ref, rows_ref):
    def body(b):
        cols = block(b, width)
        hot = mid_ref[:, cols]
        rows_ref[:, cols] = dot(second, jnp.concatenate([hot, hot], axis=0))

    for_blocks(mid_ref.shape[1] // width, body)


def half_picks(state_ref, p, gate, width, hot_ref, rows_ref, picked_ref, send_ref, scale):
    size = gate.shape[0] // 2
    rows = state_ref.shape[1] // 2
    slabs = rows // size
    real = state_ref[p, pl.ds(0, rows, stride=2), :]
    imag = state_ref[p, pl.ds(1, rows, stride=2), :]
    xh, xl = split(jnp.concatenate([real, imag], axis=1))
    first = dot(jnp.concatenate([xh, xl, xh], axis=1), gate, ((1,), (1,)))
    parts = [
        jnp.concatenate(
            [first[h * size : (h + 1) * size, c * size : (c + 1) * size] for h in range(slabs)], axis=1
        )
        for c in range(2)
    ]
    high, low = split(jnp.concatenate(parts, axis=0))
    picked_ref[: 2 * size, :] = high
    picked_ref[2 * size :, :] = low

    def body(b):
        cols = block(b, width)
        found = dot(picked_ref[...], hot_ref[:, cols])
        found = found[: 2 * size] + found[2 * size :]
        fr, fi = found[:size], found[size:]
        vr, vi = rows_ref[:size, cols], rows_ref[size:, cols]
        out_r = jnp.sum(vr * fr - vi * fi, axis=0, keepdims=True)
        out_i = jnp.sum(vr * fi + vi * fr, axis=0, keepdims=True)
        lanes = width // 128
        send_ref[b, p] = (
            jnp.concatenate(
                [o[:, k * 128 : (k + 1) * 128] for o in (out_r, out_i) for k in range(lanes)], axis=0
            )
            * scale
        )

    for_blocks(hot_ref.shape[1] // width, body)


def kernel(
    counts,
    left_ref,
    right_ref,
    gates_ref,
    left_index_ref,
    right_index_ref,
    out_ref,
    left_buf,
    right_buf,
    gates_buf,
    index_l,
    index_r,
    hot_l,
    hot_r,
    mid_l,
    mid_r,
    second_l,
    second_r,
    picked,
    send_l,
    send_r,
    recv_l,
    recv_r,
    load_sem,
    send_sem,
    recv_sem,
):
    row_count, col_count, sub_count = counts
    group = col_count * sub_count
    n = row_count * group
    size = gates_buf.shape[-1]
    held = left_buf.shape[0]
    slabs = left_buf.shape[1] // 2 // size
    tile_l = index_l.shape[1] // row_count
    tile_r = index_r.shape[1] // group
    r, c, s = lax.axis_index("rows"), lax.axis_index("cols"), lax.axis_index("sub")
    mine = c * sub_count + s
    me = r * group + mine

    loads = [
        pltpu.make_async_copy(src, dst, load_sem.at[i])
        for i, (src, dst) in enumerate(
            [
                (left_index_ref, index_l),
                (right_index_ref, index_r),
                (gates_ref, gates_buf),
                (left_ref, left_buf),
                (right_ref, right_buf),
            ]
        )
    ]
    for load in loads:
        load.start()

    def each_peer(act):
        if n <= 16:
            rows = [lax.rem(r + k, row_count) for k in range(row_count)]
            cols = [lax.rem(c + k, col_count) for k in range(col_count)]
            subs = [lax.rem(s + k, sub_count) for k in range(sub_count)]
            for i in reversed(range(n)):
                a, b, d = i // group, i // sub_count % col_count, i % sub_count
                if i:
                    act(rows[a], cols[b], subs[d])
        else:

            def step(offset, carry):
                d = lax.rem(me + offset, n)
                act(lax.div(d, group), lax.rem(lax.div(d, sub_count), col_count), lax.rem(d, sub_count))
                return carry

            lax.fori_loop(1, n, step, 0)

    barrier = pltpu.get_barrier_semaphore()

    def greet(a, b, d):
        where = {"rows": a, "cols": b, "sub": d}
        pl.semaphore_signal(barrier, inc=1, device_id=where, device_id_type=MESH)

    each_peer(greet)

    loads[0].wait()
    prepare(index_l, tile_l, size, slabs, hot_l, mid_l)
    loads[1].wait()
    prepare(index_r, tile_r, size, slabs, hot_r, mid_r)
    loads[2].wait()
    ur, ui = gates_buf[0, 0], gates_buf[0, 1]
    gh, gl = split(
        jnp.concatenate(
            [jnp.concatenate([ur, -ui], axis=1), jnp.concatenate([ui, ur], axis=1)], axis=0
        )
    )
    gate = jnp.concatenate([gh, gh, gl], axis=1)
    second = jnp.concatenate(
        split(jnp.concatenate([gates_buf[1, 0].T, gates_buf[1, 1].T], axis=0)), axis=1
    )
    gather_rows(second, tile_l, mid_l, second_l)
    gather_rows(second, tile_r, mid_r, second_r)

    def push(send, recv, which):
        def act(a, b, d):
            pltpu.make_async_remote_copy(
                src_ref=send.at[a if which == 0 else b * sub_count + d],
                dst_ref=recv.at[pl.ds(me * held, held)],
                send_sem=send_sem.at[which],
                recv_sem=recv_sem.at[which],
                device_id={"rows": a, "cols": b, "sub": d},
                device_id_type=MESH,
            ).start()

        each_peer(act)
        recv[pl.ds(me * held, held)] = send[r if which == 0 else mine]

    scale = 1.0 / math.sqrt(n * held)
    loads[3].wait()
    for p in range(held):
        half_picks(left_buf, p, gate, tile_l, hot_l, second_l, picked, send_l, scale)
    pl.semaphore_wait(barrier, n - 1)
    push(send_l, recv_l, 0)
    loads[4].wait()
    for p in range(held):
        half_picks(right_buf, p, gate, tile_r, hot_r, second_r, picked, send_r, 1.0)
    push(send_r, recv_r, 1)

    def take(recv):
        rows = recv.shape[1]
        flat = recv.reshape(recv.shape[0] * rows, 128)
        pieces = [flat[pl.ds(t, recv.shape[0], stride=rows), :] for t in range(rows)]
        return [jnp.concatenate(pieces[k : k + rows // 2], axis=1) for k in (0, rows // 2)]

    def await_bytes(ref, sem):
        pltpu.make_async_copy(ref, ref, sem).wait()

    others = pl.ds(0, (n - 1) * held)
    await_bytes(recv_l.at[others], recv_sem.at[0])
    lr, li = take(recv_l)
    lh, ll = split(jnp.concatenate([lr, li], axis=0))
    left = jnp.concatenate([lh, lh, ll], axis=0)
    await_bytes(recv_r.at[others], recv_sem.at[1])
    rr, ri = take(recv_r)
    rh, rl = split(
        jnp.concatenate(
            [jnp.concatenate([rr, -ri], axis=0), jnp.concatenate([ri, rr], axis=0)], axis=1
        )
    )
    right = jnp.concatenate([rh, rl, rh], axis=0)
    result = dot(left, right, ((0,), (0,)))
    out_ref[0] = result[:, :tile_r]
    out_ref[1] = result[:, tile_r:]
    await_bytes(recv_l.at[others], send_sem.at[0])
    await_bytes(recv_r.at[others], send_sem.at[1])


def per_device(counts, left_states, right_states, gates, left_index, right_index):
    row_count, col_count, sub_count = counts
    group = col_count * sub_count
    n = row_count * group
    size = gates.shape[-1]
    held = left_states.shape[0]
    nleft, nright = left_index.shape[0], right_index.shape[0]
    tile_l, tile_r = nleft // row_count, nright // group
    slab = left_states.shape[2]

    def rows_of(states):
        return states.reshape(held, 2, slab // size, size).transpose(0, 2, 1, 3).reshape(held, -1, size)

    hbm = pl.BlockSpec(memory_space=pltpu.HBM)
    rows = slab // size
    return pl.pallas_call(
        functools.partial(kernel, counts),
        out_shape=jax.ShapeDtypeStruct((2, tile_l, tile_r), F32),
        in_specs=[hbm] * 5,
        out_specs=pl.BlockSpec(memory_space=pltpu.VMEM),
        scratch_shapes=[
            pltpu.VMEM((held, 2 * rows, size), F32),
            pltpu.VMEM((held, 2 * rows, size), F32),
            pltpu.VMEM(gates.shape, F32),
            pltpu.VMEM((1, nleft), jnp.int32),
            pltpu.VMEM((1, nright), jnp.int32),
            pltpu.VMEM((rows, nleft), BF16),
            pltpu.VMEM((rows, nright), BF16),
            pltpu.VMEM((size, nleft), BF16),
            pltpu.VMEM((size, nright), BF16),
            pltpu.VMEM((2 * size, nleft), F32),
            pltpu.VMEM((2 * size, nright), F32),
            pltpu.VMEM((4 * size, rows), BF16),
            pltpu.VMEM((row_count, held, 2 * tile_l // 128, 128), F32),
            pltpu.VMEM((group, held, 2 * tile_r // 128, 128), F32),
            pltpu.VMEM((n * held, 2 * tile_l // 128, 128), F32),
            pltpu.VMEM((n * held, 2 * tile_r // 128, 128), F32),
            pltpu.SemaphoreType.DMA((5,)),
            pltpu.SemaphoreType.DMA((2,)),
            pltpu.SemaphoreType.DMA((2,)),
        ],
        compiler_params=pltpu.CompilerParams(
            collective_id=0, has_side_effects=True, vmem_limit_bytes=48 * 1024 * 1024
        ),
    )(
        *(
            pltpu.with_memory_space_constraint(x, pltpu.HBM)
            for x in (
                rows_of(left_states),
                rows_of(right_states),
                gates,
                left_index.reshape(1, nleft),
                right_index.reshape(1, nright),
            )
        )
    )


def solution(mesh):
    counts = tuple(mesh.shape[a] for a in ("rows", "cols", "sub"))
    return jax.shard_map(
        functools.partial(per_device, counts),
        mesh=mesh,
        in_specs=(
            P(("parts", "rows", "cols", "sub"), None, None),
            P(("parts", "rows", "cols", "sub"), None, None),
            P("parts", None, None, None),
            P("parts"),
            P("parts"),
        ),
        out_specs=P("parts", "rows", ("cols", "sub")),
        check_vma=False,
    )
```

```python
import functools
import math

import jax
import jax.numpy as jnp
from jax import lax
from jax.experimental import pallas as pl
from jax.experimental.pallas import tpu as pltpu
from jax.sharding import PartitionSpec as P

MESH = pl.DeviceIdType.MESH
BF16 = jnp.bfloat16
F32 = jnp.float32


def split(x):
    high = x.astype(BF16)
    return high, (x - high.astype(F32)).astype(BF16)


def dot(a, b, dims=((1,), (0,))):
    return lax.dot_general(a, b, (dims, ((), ())), preferred_element_type=F32)


def for_blocks(count, body):
    if count <= 4:
        for b in range(count):
            body(b)
    else:

        def step(b, carry):
            body(b)
            return carry

        lax.fori_loop(0, count, step, 0)


def block(b, width):
    start = b * width
    return pl.ds(start if isinstance(start, int) else pl.multiple_of(start, width), width)


def prepare(index_ref, width, size, slabs, hot_ref, mid_ref):
    shift = size.bit_length() - 1

    def body(b):
        cols = block(b, width)
        index = index_ref[:, cols]
        column = ((index >> (2 * shift)) << shift) | (index & (size - 1))
        mid = (index >> shift) & (size - 1)
        spot = lax.broadcasted_iota(jnp.int32, (slabs * size, width), 0)
        hot_ref[:, cols] = jnp.where(spot == column, 1.0, 0.0).astype(BF16)
        spot = lax.broadcasted_iota(jnp.int32, (size, width), 0)
        mid_ref[:, cols] = jnp.where(spot == mid, 1.0, 0.0).astype(BF16)

    for_blocks(index_ref.shape[1] // width, body)


def gather_rows(second, width, mid_ref, rows_ref):
    def body(b):
        cols = block(b, width)
        hot = mid_ref[:, cols]
        rows_ref[:, cols] = dot(second, jnp.concatenate([hot, hot], axis=0))

    for_blocks(mid_ref.shape[1] // width, body)


def half_picks(state_ref, gate, width, hot_ref, rows_ref, picked_ref, emit):
    size = gate.shape[1] // 2
    rows = state_ref.shape[0] // 2
    slabs = rows // size
    real = state_ref[pl.ds(0, rows, stride=2), :]
    imag = state_ref[pl.ds(1, rows, stride=2), :]
    xh, xl = split(jnp.concatenate([real, imag], axis=1))
    first = dot(jnp.concatenate([xh, xl, xh], axis=1), gate)
    parts = [
        jnp.concatenate(
            [first[h * size : (h + 1) * size, c * size : (c + 1) * size] for h in range(slabs)], axis=1
        )
        for c in range(2)
    ]
    high, low = split(jnp.concatenate(parts, axis=0))
    picked_ref[: 2 * size, :] = high
    picked_ref[2 * size :, :] = low

    def body(b):
        cols = block(b, width)
        found = dot(picked_ref[...], hot_ref[:, cols])
        found = found[: 2 * size] + found[2 * size :]
        fr, fi = found[:size], found[size:]
        vr, vi = rows_ref[:size, cols], rows_ref[size:, cols]
        out_r = jnp.sum(vr * fr - vi * fi, axis=0, keepdims=True)
        out_i = jnp.sum(vr * fi + vi * fr, axis=0, keepdims=True)
        lanes = width // 128
        emit(
            b,
            jnp.concatenate(
                [o[:, k * 128 : (k + 1) * 128] for o in (out_r, out_i) for k in range(lanes)], axis=0
            ),
        )

    for_blocks(hot_ref.shape[1] // width, body)


def kernel(
    counts,
    left_ref,
    right_ref,
    gates_ref,
    left_index_ref,
    right_index_ref,
    out_ref,
    left_buf,
    right_buf,
    gates_buf,
    index_l,
    index_r,
    hot_l,
    hot_r,
    mid_l,
    mid_r,
    second_l,
    second_r,
    picked,
    send,
    recv,
    load_sem,
    send_sem,
    recv_sem,
):
    row_count, col_count, sub_count = counts
    group = col_count * sub_count
    n = row_count * group
    size = gates_buf.shape[-1]
    held = left_buf.shape[0]
    slabs = left_buf.shape[1] // 2 // size
    tile_l = index_l.shape[1] // row_count
    tile_r = index_r.shape[1] // group
    r, c, s = lax.axis_index("rows"), lax.axis_index("cols"), lax.axis_index("sub")
    mine = c * sub_count + s
    me = r * group + mine
    rows_l, rows_r = 2 * tile_l // 128, 2 * tile_r // 128
    unit = rows_l + rows_r
    slot = held * unit

    loads = [
        pltpu.make_async_copy(src, dst, load_sem.at[i])
        for i, (src, dst) in enumerate(
            [
                (left_index_ref, index_l),
                (right_index_ref, index_r),
                (gates_ref, gates_buf),
            ]
            + [
                (src.at[:, pl.ds(h * 2 * size, 2 * size)], dst.at[:, pl.ds(h * 2 * size, 2 * size)])
                for src, dst in ((left_ref, left_buf), (right_ref, right_buf))
                for h in range(slabs)
            ]
        )
    ]
    for load in loads:
        load.start()

    def each_peer(act):
        if n <= 16:
            rows = [lax.rem(r + k, row_count) for k in range(row_count)]
            cols = [lax.rem(c + k, col_count) for k in range(col_count)]
            subs = [lax.rem(s + k, sub_count) for k in range(sub_count)]
            for i in reversed(range(n)):
                a, b, d = i // group, i // sub_count % col_count, i % sub_count
                if i:
                    act(rows[a], cols[b], subs[d])
        else:

            def step(offset, carry):
                d = lax.rem(me + offset, n)
                act(lax.div(d, group), lax.rem(lax.div(d, sub_count), col_count), lax.rem(d, sub_count))
                return carry

            lax.fori_loop(1, n, step, 0)

    barrier = pltpu.get_barrier_semaphore()

    def greet(a, b, d):
        where = {"rows": a, "cols": b, "sub": d}
        pl.semaphore_signal(barrier, inc=1, device_id=where, device_id_type=MESH)

    each_peer(greet)

    loads[0].wait()
    prepare(index_l, tile_l, size, slabs, hot_l, mid_l)
    loads[1].wait()
    prepare(index_r, tile_r, size, slabs, hot_r, mid_r)
    loads[2].wait()
    ur, ui = gates_buf[0, 0], gates_buf[0, 1]
    ur, ui = ur.T, ui.T
    gh, gl = split(
        jnp.concatenate(
            [jnp.concatenate([ur, ui], axis=1), jnp.concatenate([-ui, ur], axis=1)], axis=0
        )
    )
    gate = jnp.concatenate([gh, gh, gl], axis=0)
    second = jnp.concatenate(
        split(jnp.concatenate([gates_buf[1, 0].T, gates_buf[1, 1].T], axis=0)), axis=1
    )
    gather_rows(second, tile_l, mid_l, second_l)
    gather_rows(second, tile_r, mid_r, second_r)

    scale = 1.0 / math.sqrt(n * held)
    for load in loads[3:]:
        load.wait()
    for p in range(held):

        def emit_left(b, rows, p=p):
            rows = rows * scale
            for g in range(group):
                send[b * group + g, p * unit : p * unit + rows_l, :] = rows

        def emit_right(b, rows, p=p):
            for a in range(row_count):
                send[a * group + b, p * unit + rows_l : (p + 1) * unit, :] = rows

        half_picks(left_buf.at[p], gate, tile_l, hot_l, second_l, picked.at[0], emit_left)
        half_picks(right_buf.at[p], gate, tile_r, hot_r, second_r, picked.at[1], emit_right)

    pl.semaphore_wait(barrier, n - 1)
    spot = pl.ds(pl.multiple_of(me * slot, slot), slot)

    def push(a, b, d):
        pltpu.make_async_remote_copy(
            src_ref=send.at[a * group + b * sub_count + d],
            dst_ref=recv.at[spot, :],
            send_sem=send_sem,
            recv_sem=recv_sem,
            device_id={"rows": a, "cols": b, "sub": d},
            device_id_type=MESH,
        ).start()

    each_peer(push)
    recv[spot, :] = send[me]
    others = recv.at[pl.ds(0, (n - 1) * slot), :]
    pltpu.make_async_copy(others, others, recv_sem).wait()

    def take(start, rows):
        return jnp.concatenate(
            [recv[pl.ds(start + t, n * held, stride=unit), :] for t in range(rows)], axis=1
        )

    lr, li = take(0, rows_l // 2), take(rows_l // 2, rows_l // 2)
    rr, ri = take(rows_l, rows_r // 2), take(rows_l + rows_r // 2, rows_r // 2)
    lh, ll = split(jnp.concatenate([lr, li], axis=0))
    rh, rl = split(
        jnp.concatenate(
            [jnp.concatenate([rr, -ri], axis=0), jnp.concatenate([ri, rr], axis=0)], axis=1
        )
    )
    left = jnp.concatenate([lh, lh, ll], axis=0)
    right = jnp.concatenate([rh, rl, rh], axis=0)
    result = dot(left, right, ((0,), (0,)))
    out_ref[0] = result[:, :tile_r]
    out_ref[1] = result[:, tile_r:]
    pltpu.make_async_copy(others, others, send_sem).wait()


def per_device(counts, left_states, right_states, gates, left_index, right_index):
    row_count, col_count, sub_count = counts
    group = col_count * sub_count
    n = row_count * group
    size = gates.shape[-1]
    held = left_states.shape[0]
    nleft, nright = left_index.shape[0], right_index.shape[0]
    tile_l, tile_r = nleft // row_count, nright // group
    unit = 2 * (tile_l + tile_r) // 128
    slab = left_states.shape[2]

    def rows_of(states):
        return states.reshape(held, 2, slab // size, size).transpose(0, 2, 1, 3).reshape(held, -1, size)

    hbm = pl.BlockSpec(memory_space=pltpu.HBM)
    rows = slab // size
    return pl.pallas_call(
        functools.partial(kernel, counts),
        out_shape=jax.ShapeDtypeStruct((2, tile_l, tile_r), F32),
        in_specs=[hbm] * 5,
        out_specs=pl.BlockSpec(memory_space=pltpu.VMEM),
        scratch_shapes=[
            pltpu.VMEM((held, 2 * rows, size), F32),
            pltpu.VMEM((held, 2 * rows, size), F32),
            pltpu.VMEM(gates.shape, F32),
            pltpu.VMEM((1, nleft), jnp.int32),
            pltpu.VMEM((1, nright), jnp.int32),
            pltpu.VMEM((rows, nleft), BF16),
            pltpu.VMEM((rows, nright), BF16),
            pltpu.VMEM((size, nleft), BF16),
            pltpu.VMEM((size, nright), BF16),
            pltpu.VMEM((2 * size, nleft), F32),
            pltpu.VMEM((2 * size, nright), F32),
            pltpu.VMEM((2, 4 * size, rows), BF16),
            pltpu.VMEM((n, held * unit, 128), F32),
            pltpu.VMEM((n * held * unit, 128), F32),
            pltpu.SemaphoreType.DMA((3 + 2 * (rows // size),)),
            pltpu.SemaphoreType.DMA,
            pltpu.SemaphoreType.DMA,
        ],
        compiler_params=pltpu.CompilerParams(
            collective_id=0, has_side_effects=True, vmem_limit_bytes=48 * 1024 * 1024
        ),
    )(
        *(
            pltpu.with_memory_space_constraint(x, pltpu.HBM)
            for x in (
                rows_of(left_states),
                rows_of(right_states),
                gates,
                left_index.reshape(1, nleft),
                right_index.reshape(1, nright),
            )
        )
    )


def solution(mesh):
    counts = tuple(mesh.shape[a] for a in ("rows", "cols", "sub"))
    return jax.shard_map(
        functools.partial(per_device, counts),
        mesh=mesh,
        in_specs=(
            P(("parts", "rows", "cols", "sub"), None, None),
            P(("parts", "rows", "cols", "sub"), None, None),
            P("parts", None, None, None),
            P("parts"),
            P("parts"),
        ),
        out_specs=P("parts", "rows", ("cols", "sub")),
        check_vma=False,
    )
```

```python
import functools
import math

import jax
import jax.numpy as jnp
from jax import lax
from jax.experimental import pallas as pl
from jax.experimental.pallas import tpu as pltpu
from jax.sharding import PartitionSpec as P

MESH = pl.DeviceIdType.MESH
BF16 = jnp.bfloat16
F32 = jnp.float32


def split(x):
    high = x.astype(BF16)
    return high, (x - high.astype(F32)).astype(BF16)


def dot(a, b, dims=((1,), (0,))):
    return lax.dot_general(a, b, (dims, ((), ())), preferred_element_type=F32)


def for_blocks(count, body):
    if count <= 8:
        for b in range(count):
            body(b)
    else:

        def step(b, carry):
            body(b)
            return carry

        lax.fori_loop(0, count, step, 0)


def block(b, width):
    start = b * width
    return pl.ds(start if isinstance(start, int) else pl.multiple_of(start, width), width)


def lanes(values, index):
    spread = jnp.broadcast_to(index, (values.shape[0], index.shape[1]))
    return jnp.take_along_axis(values, spread, axis=1, mode="promise_in_bounds")


def apply_first(state_ref, gate, first_ref):
    rows = state_ref.shape[0] // 2
    real = state_ref[pl.ds(0, rows, stride=2), :]
    imag = state_ref[pl.ds(1, rows, stride=2), :]
    xh, xl = split(jnp.concatenate([real, imag], axis=1))
    first_ref[...] = dot(jnp.concatenate([xh, xl, xh], axis=1), gate)


def gather_rows(second, index_ref, rows_ref):
    size = second[0].shape[0]
    shift = size.bit_length() - 1

    def body(b):
        cols = block(b, size)
        mid = (index_ref[:, cols] >> shift) & (size - 1)
        rows_ref[:size, cols] = lanes(second[0], mid)
        rows_ref[size:, cols] = lanes(second[1], mid)

    for_blocks(index_ref.shape[1] // size, body)


def half_picks(first_ref, width, index_ref, rows_ref, emit):
    size = first_ref.shape[1] // 2
    shift = size.bit_length() - 1
    slabs = first_ref.shape[0] // size

    def body(b):
        out_r, out_i = [], []
        for k in range(width // size):
            cols = block(b * (width // size) + k, size)
            index = index_ref[:, cols]
            low = index & (size - 1)
            slab = jnp.broadcast_to(index >> (2 * shift), (size, size))
            found = []
            for c in range(2):
                part = [
                    lanes(first_ref[h * size : (h + 1) * size, c * size : (c + 1) * size], low)
                    for h in range(slabs)
                ]
                value = part[0]
                for h in range(1, slabs):
                    value = jnp.where(slab == h, part[h], value)
                found.append(value)
            fr, fi = found
            vr, vi = rows_ref[:size, cols], rows_ref[size:, cols]
            out_r.append(jnp.sum(vr * fr - vi * fi, axis=0, keepdims=True))
            out_i.append(jnp.sum(vr * fi + vi * fr, axis=0, keepdims=True))
        emit(b, jnp.concatenate(out_r + out_i, axis=0))

    for_blocks(index_ref.shape[1] // width, body)


def kernel(
    counts,
    left_ref,
    right_ref,
    gates_ref,
    left_index_ref,
    right_index_ref,
    out_ref,
    left_buf,
    right_buf,
    gates_buf,
    index_l,
    index_r,
    second_l,
    second_r,
    picked,
    send,
    recv,
    load_sem,
    send_sem,
    recv_sem,
):
    row_count, col_count, sub_count = counts
    group = col_count * sub_count
    n = row_count * group
    size = gates_buf.shape[-1]
    held = left_buf.shape[0]
    slabs = left_buf.shape[1] // 2 // size
    tile_l = index_l.shape[1] // row_count
    tile_r = index_r.shape[1] // group
    r, c, s = lax.axis_index("rows"), lax.axis_index("cols"), lax.axis_index("sub")
    mine = c * sub_count + s
    me = r * group + mine
    rows_l, rows_r = 2 * tile_l // 128, 2 * tile_r // 128
    unit = rows_l + rows_r
    slot = held * unit

    loads = [
        pltpu.make_async_copy(src, dst, load_sem.at[i])
        for i, (src, dst) in enumerate(
            [
                (left_index_ref, index_l),
                (right_index_ref, index_r),
                (gates_ref, gates_buf),
            ]
            + [
                (src.at[:, pl.ds(h * 2 * size, 2 * size)], dst.at[:, pl.ds(h * 2 * size, 2 * size)])
                for src, dst in ((left_ref, left_buf), (right_ref, right_buf))
                for h in range(slabs)
            ]
        )
    ]
    for load in loads:
        load.start()

    def each_peer(act):
        if n <= 16:
            rows = [lax.rem(r + k, row_count) for k in range(row_count)]
            cols = [lax.rem(c + k, col_count) for k in range(col_count)]
            subs = [lax.rem(s + k, sub_count) for k in range(sub_count)]
            for i in reversed(range(n)):
                a, b, d = i // group, i // sub_count % col_count, i % sub_count
                if i:
                    act(rows[a], cols[b], subs[d])
        else:

            def step(offset, carry):
                d = lax.rem(me + offset, n)
                act(lax.div(d, group), lax.rem(lax.div(d, sub_count), col_count), lax.rem(d, sub_count))
                return carry

            lax.fori_loop(1, n, step, 0)

    barrier = pltpu.get_barrier_semaphore()

    def greet(a, b, d):
        where = {"rows": a, "cols": b, "sub": d}
        pl.semaphore_signal(barrier, inc=1, device_id=where, device_id_type=MESH)

    each_peer(greet)

    loads[0].wait()
    loads[1].wait()
    loads[2].wait()
    ur, ui = gates_buf[0, 0], gates_buf[0, 1]
    ur, ui = ur.T, ui.T
    gh, gl = split(
        jnp.concatenate(
            [jnp.concatenate([ur, ui], axis=1), jnp.concatenate([-ui, ur], axis=1)], axis=0
        )
    )
    gate = jnp.concatenate([gh, gh, gl], axis=0)
    second = (gates_buf[1, 0].T, gates_buf[1, 1].T)
    gather_rows(second, index_l, second_l)
    gather_rows(second, index_r, second_r)

    scale = 1.0 / math.sqrt(n * held)
    for load in loads[3:]:
        load.wait()
    for p in range(held):

        def emit_left(b, rows, p=p):
            rows = rows * scale
            for g in range(group):
                send[b * group + g, p * unit : p * unit + rows_l, :] = rows

        def emit_right(b, rows, p=p):
            for a in range(row_count):
                send[a * group + b, p * unit + rows_l : (p + 1) * unit, :] = rows

        apply_first(left_buf.at[p], gate, picked.at[0])
        apply_first(right_buf.at[p], gate, picked.at[1])
        half_picks(picked.at[0], tile_l, index_l, second_l, emit_left)
        half_picks(picked.at[1], tile_r, index_r, second_r, emit_right)

    pl.semaphore_wait(barrier, n - 1)
    spot = pl.ds(pl.multiple_of(me * slot, slot), slot)

    def push(a, b, d):
        pltpu.make_async_remote_copy(
            src_ref=send.at[a * group + b * sub_count + d],
            dst_ref=recv.at[spot, :],
            send_sem=send_sem,
            recv_sem=recv_sem,
            device_id={"rows": a, "cols": b, "sub": d},
            device_id_type=MESH,
        ).start()

    each_peer(push)
    recv[spot, :] = send[me]
    others = recv.at[pl.ds(0, (n - 1) * slot), :]
    pltpu.make_async_copy(others, others, recv_sem).wait()

    def take(start, rows):
        return jnp.concatenate(
            [recv[pl.ds(start + t, n * held, stride=unit), :] for t in range(rows)], axis=1
        )

    lr, li = take(0, rows_l // 2), take(rows_l // 2, rows_l // 2)
    rr, ri = take(rows_l, rows_r // 2), take(rows_l + rows_r // 2, rows_r // 2)
    lh, ll = split(jnp.concatenate([lr, li], axis=0))
    rh, rl = split(
        jnp.concatenate(
            [jnp.concatenate([rr, -ri], axis=0), jnp.concatenate([ri, rr], axis=0)], axis=1
        )
    )
    left = jnp.concatenate([lh, lh, ll], axis=0)
    right = jnp.concatenate([rh, rl, rh], axis=0)
    result = dot(left, right, ((0,), (0,)))
    out_ref[0] = result[:, :tile_r]
    out_ref[1] = result[:, tile_r:]
    pltpu.make_async_copy(others, others, send_sem).wait()


def per_device(counts, left_states, right_states, gates, left_index, right_index):
    row_count, col_count, sub_count = counts
    group = col_count * sub_count
    n = row_count * group
    size = gates.shape[-1]
    held = left_states.shape[0]
    nleft, nright = left_index.shape[0], right_index.shape[0]
    tile_l, tile_r = nleft // row_count, nright // group
    unit = 2 * (tile_l + tile_r) // 128
    slab = left_states.shape[2]

    def rows_of(states):
        return states.reshape(held, 2, slab // size, size).transpose(0, 2, 1, 3).reshape(held, -1, size)

    hbm = pl.BlockSpec(memory_space=pltpu.HBM)
    rows = slab // size
    return pl.pallas_call(
        functools.partial(kernel, counts),
        out_shape=jax.ShapeDtypeStruct((2, tile_l, tile_r), F32),
        in_specs=[hbm] * 5,
        out_specs=pl.BlockSpec(memory_space=pltpu.VMEM),
        scratch_shapes=[
            pltpu.VMEM((held, 2 * rows, size), F32),
            pltpu.VMEM((held, 2 * rows, size), F32),
            pltpu.VMEM(gates.shape, F32),
            pltpu.VMEM((1, nleft), jnp.int32),
            pltpu.VMEM((1, nright), jnp.int32),
            pltpu.VMEM((2 * size, nleft), F32),
            pltpu.VMEM((2 * size, nright), F32),
            pltpu.VMEM((2, rows, 2 * size), F32),
            pltpu.VMEM((n, held * unit, 128), F32),
            pltpu.VMEM((n * held * unit, 128), F32),
            pltpu.SemaphoreType.DMA((3 + 2 * (rows // size),)),
            pltpu.SemaphoreType.DMA,
            pltpu.SemaphoreType.DMA,
        ],
        compiler_params=pltpu.CompilerParams(
            collective_id=0, has_side_effects=True, vmem_limit_bytes=48 * 1024 * 1024
        ),
    )(
        *(
            pltpu.with_memory_space_constraint(x, pltpu.HBM)
            for x in (
                rows_of(left_states),
                rows_of(right_states),
                gates,
                left_index.reshape(1, nleft),
                right_index.reshape(1, nright),
            )
        )
    )


def solution(mesh):
    counts = tuple(mesh.shape[a] for a in ("rows", "cols", "sub"))
    return jax.shard_map(
        functools.partial(per_device, counts),
        mesh=mesh,
        in_specs=(
            P(("parts", "rows", "cols", "sub"), None, None),
            P(("parts", "rows", "cols", "sub"), None, None),
            P("parts", None, None, None),
            P("parts"),
            P("parts"),
        ),
        out_specs=P("parts", "rows", ("cols", "sub")),
        check_vma=False,
    )
```

```python
import functools
import math

import jax
import jax.numpy as jnp
from jax import lax
from jax.experimental import pallas as pl
from jax.experimental.pallas import tpu as pltpu
from jax.sharding import PartitionSpec as P

MESH = pl.DeviceIdType.MESH
BF16 = jnp.bfloat16
F32 = jnp.float32


def split(x):
    high = x.astype(BF16)
    return high, (x - high.astype(F32)).astype(BF16)


def dot(a, b, dims=((1,), (0,))):
    return lax.dot_general(a, b, (dims, ((), ())), preferred_element_type=F32)


def for_blocks(count, body):
    if count <= 4:
        for b in range(count):
            body(b)
    else:

        def step(b, carry):
            body(b)
            return carry

        lax.fori_loop(0, count, step, 0)


def block(b, width):
    start = b * width
    return pl.ds(start if isinstance(start, int) else pl.multiple_of(start, width), width)


def prepare(index_ref, width, size, slabs, hot_ref):
    shift = size.bit_length() - 1

    def body(b):
        cols = block(b, width)
        index = index_ref[:, cols]
        column = ((index >> (2 * shift)) << shift) | (index & (size - 1))
        spot = lax.broadcasted_iota(jnp.int32, (slabs * size, width), 0)
        hot_ref[:, cols] = jnp.where(spot == column, 1.0, 0.0).astype(BF16)

    for_blocks(index_ref.shape[1] // width, body)


def gather_rows(second, index):
    size = second.shape[0]
    shift = size.bit_length() - 1
    pieces = []
    for k in range(index.shape[1] // size):
        mid = (index[:, k * size : (k + 1) * size] >> shift) & (size - 1)
        spread = jnp.broadcast_to(mid, (size, size))
        pieces.append(jnp.take_along_axis(second, spread, axis=1, mode="promise_in_bounds"))
    return jnp.concatenate(pieces, axis=1)


def half_picks(state_ref, gate, width, hot_ref, index_ref, second_ref, picked_ref, emit):
    size = gate.shape[1] // 2
    rows = state_ref.shape[0] // 2
    slabs = rows // size
    real = state_ref[pl.ds(0, rows, stride=2), :]
    imag = state_ref[pl.ds(1, rows, stride=2), :]
    xh, xl = split(jnp.concatenate([real, imag], axis=1))
    first = dot(jnp.concatenate([xh, xl, xh], axis=1), gate)
    parts = [
        jnp.concatenate(
            [first[h * size : (h + 1) * size, c * size : (c + 1) * size] for h in range(slabs)], axis=1
        )
        for c in range(2)
    ]
    high, low = split(jnp.concatenate(parts, axis=0))
    picked_ref[: 2 * size, :] = high
    picked_ref[2 * size :, :] = low

    def body(b):
        cols = block(b, width)
        found = dot(picked_ref[...], hot_ref[:, cols])
        found = found[: 2 * size] + found[2 * size :]
        fr, fi = found[:size], found[size:]
        index = index_ref[:, cols]
        vr, vi = gather_rows(second_ref[0], index), gather_rows(second_ref[1], index)
        out_r = jnp.sum(vr * fr - vi * fi, axis=0, keepdims=True)
        out_i = jnp.sum(vr * fi + vi * fr, axis=0, keepdims=True)
        lanes = width // 128
        emit(
            b,
            jnp.concatenate(
                [o[:, k * 128 : (k + 1) * 128] for o in (out_r, out_i) for k in range(lanes)], axis=0
            ),
        )

    for_blocks(hot_ref.shape[1] // width, body)


def kernel(
    counts,
    left_ref,
    right_ref,
    gates_ref,
    left_index_ref,
    right_index_ref,
    out_ref,
    left_buf,
    right_buf,
    gates_buf,
    index_l,
    index_r,
    hot_l,
    hot_r,
    second,
    picked,
    send,
    recv,
    load_sem,
    send_sem,
    recv_sem,
):
    row_count, col_count, sub_count = counts
    group = col_count * sub_count
    n = row_count * group
    size = gates_buf.shape[-1]
    held = left_buf.shape[0]
    slabs = left_buf.shape[1] // 2 // size
    tile_l = index_l.shape[1] // row_count
    tile_r = index_r.shape[1] // group
    r, c, s = lax.axis_index("rows"), lax.axis_index("cols"), lax.axis_index("sub")
    mine = c * sub_count + s
    me = r * group + mine
    rows_l, rows_r = 2 * tile_l // 128, 2 * tile_r // 128
    unit = rows_l + rows_r
    slot = held * unit

    loads = [
        pltpu.make_async_copy(src, dst, load_sem.at[i])
        for i, (src, dst) in enumerate(
            [
                (left_index_ref, index_l),
                (right_index_ref, index_r),
                (gates_ref, gates_buf),
            ]
            + [
                (src.at[:, pl.ds(h * 2 * size, 2 * size)], dst.at[:, pl.ds(h * 2 * size, 2 * size)])
                for src, dst in ((left_ref, left_buf), (right_ref, right_buf))
                for h in range(slabs)
            ]
        )
    ]
    for load in loads:
        load.start()

    def each_peer(act):
        if n <= 16:
            rows = [lax.rem(r + k, row_count) for k in range(row_count)]
            cols = [lax.rem(c + k, col_count) for k in range(col_count)]
            subs = [lax.rem(s + k, sub_count) for k in range(sub_count)]
            for i in reversed(range(n)):
                a, b, d = i // group, i // sub_count % col_count, i % sub_count
                if i:
                    act(rows[a], cols[b], subs[d])
        else:

            def step(offset, carry):
                d = lax.rem(me + offset, n)
                act(lax.div(d, group), lax.rem(lax.div(d, sub_count), col_count), lax.rem(d, sub_count))
                return carry

            lax.fori_loop(1, n, step, 0)

    barrier = pltpu.get_barrier_semaphore()

    def greet(a, b, d):
        where = {"rows": a, "cols": b, "sub": d}
        pl.semaphore_signal(barrier, inc=1, device_id=where, device_id_type=MESH)

    each_peer(greet)

    loads[0].wait()
    prepare(index_l, tile_l, size, slabs, hot_l)
    loads[1].wait()
    prepare(index_r, tile_r, size, slabs, hot_r)
    loads[2].wait()
    ur, ui = gates_buf[0, 0], gates_buf[0, 1]
    ur, ui = ur.T, ui.T
    gh, gl = split(
        jnp.concatenate(
            [jnp.concatenate([ur, ui], axis=1), jnp.concatenate([-ui, ur], axis=1)], axis=0
        )
    )
    gate = jnp.concatenate([gh, gh, gl], axis=0)
    second[0] = gates_buf[1, 0].T
    second[1] = gates_buf[1, 1].T

    scale = 1.0 / math.sqrt(n * held)
    for load in loads[3:]:
        load.wait()
    for p in range(held):

        def emit_left(b, rows, p=p):
            rows = rows * scale
            for g in range(group):
                send[b * group + g, p * unit : p * unit + rows_l, :] = rows

        def emit_right(b, rows, p=p):
            for a in range(row_count):
                send[a * group + b, p * unit + rows_l : (p + 1) * unit, :] = rows

        half_picks(left_buf.at[p], gate, tile_l, hot_l, index_l, second, picked.at[0], emit_left)
        half_picks(right_buf.at[p], gate, tile_r, hot_r, index_r, second, picked.at[1], emit_right)

    pl.semaphore_wait(barrier, n - 1)
    spot = pl.ds(pl.multiple_of(me * slot, slot), slot)

    def push(a, b, d):
        pltpu.make_async_remote_copy(
            src_ref=send.at[a * group + b * sub_count + d],
            dst_ref=recv.at[spot, :],
            send_sem=send_sem,
            recv_sem=recv_sem,
            device_id={"rows": a, "cols": b, "sub": d},
            device_id_type=MESH,
        ).start()

    each_peer(push)
    recv[spot, :] = send[me]
    others = recv.at[pl.ds(0, (n - 1) * slot), :]
    pltpu.make_async_copy(others, others, recv_sem).wait()

    def take(start, rows):
        return jnp.concatenate(
            [recv[pl.ds(start + t, n * held, stride=unit), :] for t in range(rows)], axis=1
        )

    lr, li = take(0, rows_l // 2), take(rows_l // 2, rows_l // 2)
    rr, ri = take(rows_l, rows_r // 2), take(rows_l + rows_r // 2, rows_r // 2)
    lh, ll = split(jnp.concatenate([lr, li], axis=0))
    rh, rl = split(
        jnp.concatenate(
            [jnp.concatenate([rr, -ri], axis=0), jnp.concatenate([ri, rr], axis=0)], axis=1
        )
    )
    left = jnp.concatenate([lh, lh, ll], axis=0)
    right = jnp.concatenate([rh, rl, rh], axis=0)
    result = dot(left, right, ((0,), (0,)))
    out_ref[0] = result[:, :tile_r]
    out_ref[1] = result[:, tile_r:]
    pltpu.make_async_copy(others, others, send_sem).wait()


def per_device(counts, left_states, right_states, gates, left_index, right_index):
    row_count, col_count, sub_count = counts
    group = col_count * sub_count
    n = row_count * group
    size = gates.shape[-1]
    held = left_states.shape[0]
    nleft, nright = left_index.shape[0], right_index.shape[0]
    tile_l, tile_r = nleft // row_count, nright // group
    unit = 2 * (tile_l + tile_r) // 128
    slab = left_states.shape[2]

    def rows_of(states):
        return states.reshape(held, 2, slab // size, size).transpose(0, 2, 1, 3).reshape(held, -1, size)

    hbm = pl.BlockSpec(memory_space=pltpu.HBM)
    rows = slab // size
    return pl.pallas_call(
        functools.partial(kernel, counts),
        out_shape=jax.ShapeDtypeStruct((2, tile_l, tile_r), F32),
        in_specs=[hbm] * 5,
        out_specs=pl.BlockSpec(memory_space=pltpu.VMEM),
        scratch_shapes=[
            pltpu.VMEM((held, 2 * rows, size), F32),
            pltpu.VMEM((held, 2 * rows, size), F32),
            pltpu.VMEM(gates.shape, F32),
            pltpu.VMEM((1, nleft), jnp.int32),
            pltpu.VMEM((1, nright), jnp.int32),
            pltpu.VMEM((rows, nleft), BF16),
            pltpu.VMEM((rows, nright), BF16),
            pltpu.VMEM((2, size, size), F32),
            pltpu.VMEM((2, 4 * size, rows), BF16),
            pltpu.VMEM((n, held * unit, 128), F32),
            pltpu.VMEM((n * held * unit, 128), F32),
            pltpu.SemaphoreType.DMA((3 + 2 * (rows // size),)),
            pltpu.SemaphoreType.DMA,
            pltpu.SemaphoreType.DMA,
        ],
        compiler_params=pltpu.CompilerParams(
            collective_id=0, has_side_effects=True, vmem_limit_bytes=48 * 1024 * 1024
        ),
    )(
        *(
            pltpu.with_memory_space_constraint(x, pltpu.HBM)
            for x in (
                rows_of(left_states),
                rows_of(right_states),
                gates,
                left_index.reshape(1, nleft),
                right_index.reshape(1, nright),
            )
        )
    )


def solution(mesh):
    counts = tuple(mesh.shape[a] for a in ("rows", "cols", "sub"))
    return jax.shard_map(
        functools.partial(per_device, counts),
        mesh=mesh,
        in_specs=(
            P(("parts", "rows", "cols", "sub"), None, None),
            P(("parts", "rows", "cols", "sub"), None, None),
            P("parts", None, None, None),
            P("parts"),
            P("parts"),
        ),
        out_specs=P("parts", "rows", ("cols", "sub")),
        check_vma=False,
    )
```
